128 devices in a mesh: row: 16 (over x, z), col: 8 (over y, core).
Axes of the slice: x: 4, y: 4, z: 4, core: 2. Of those that a mesh axis runs over, the one named last changes fastest.
Arguments:
- inputs: bfloat16 [1024, 12288], P('row', 'col'), may hold values from -0.1875 to 0.1875
- pre_act: bfloat16 [1024, 49152], P('col', 'row'), may hold values from -6 to 6
- grad_out: bfloat16 [1024, 49152], P('col', 'row'), may hold values from -6 to 6
- weight: bfloat16 [12288, 49152], P('col', 'row'), may hold values from -0.02734375 to 0.02734375
Outputs:
- grad_input: bfloat16 [1024, 12288], P('row', 'col')
- grad_weight: bfloat16 [12288, 49152], P('col', 'row')
The draws below stay inside these ranges and needn't reach their ends.
All inputs are finite; a program needn't handle non-finite values.
Results may differ from the reference program's by a relative error of at most 0.019.
Values may be sent and summed in bfloat16 or wider, within the bound.
No kernel may reach another device: no remote copies, remote signals or barrier semaphores. Data moves between devices by JAX's collectives and lax.ppermute only.
A program may use at most 128 MiB of HBM per device.

```python
import jax
import jax.numpy as jnp
from jax import lax

D = 12288
FF = 49152
TOKENS = 1024
N_ROW = 16


def block_scale(rng, dims, cuts, smallest, top_value):
    factor_of = 1.0
    for dim, blocks in cuts:
        steps = jax.random.uniform(jax.random.fold_in(jax.random.fold_in(rng, 6), dim), (blocks,), jnp.float32, smallest / len(cuts), top_value / len(cuts))
        factor_of = factor_of * jnp.repeat(jnp.exp(steps), dims[dim] // blocks).reshape((-1,) + (1,) * (len(dims) - 1 - dim))
    return factor_of


def centred(rng, shape, width, most, cuts=(), held_as=jnp.bfloat16):
    array = jax.random.normal(rng, shape, jnp.float32) * width
    if len(cuts) > 0:
        array = block_scale(rng, shape, cuts, -0.22, 0.18) * array
    return jnp.clip(array, min=-most, max=most).astype(held_as)


def setup_inputs(seed: int = 0) -> dict:
    key_of = jax.random.split(jax.random.key(seed), 5)
    inputs = centred(key_of[0], (TOKENS, D), (TOKENS ** -0.5), 0.1875, ((0, 16), (1, 8)))
    pre_act = centred(key_of[1], (TOKENS, FF), 1.0, 6.0, ((0, 8), (1, 16)))
    grad_out = centred(key_of[2], (TOKENS, FF), 1.0, 6.0, ((0, 8), (1, 16)))
    weight = centred(key_of[3], (D, FF), FF ** -0.5, 0.02734375, ((0, 8), (1, 16)))
    return {"inputs": inputs, "pre_act": pre_act, "grad_out": grad_out, "weight": weight}


def gelu_slope(value):
    coeff = 0.7978845608
    inner = coeff * (value + 0.044715 * value * value * value)
    tanh_u = jnp.tanh(inner)
    return 0.5 * (1.0 + tanh_u) + 0.5 * value * (1.0 - tanh_u * tanh_u) * coeff * (1.0 + 3.0 * 0.044715 * value * value)


def reference(inputs, pre_act, grad_out, weight):
    grad_hidden = (grad_out.astype(jnp.float32) * gelu_slope(pre_act.astype(jnp.float32))).astype(jnp.bfloat16)
    group = FF // N_ROW

    def add_group(index, total):
        start = (index * group).astype(jnp.int32)
        hidden_cols = lax.dynamic_slice_in_dim(grad_hidden, start, group, 1)
        weight_cols = lax.dynamic_slice_in_dim(weight, start, group, 1)
        partial_value = jnp.dot(hidden_cols, weight_cols.T, preferred_element_type=jnp.float32).astype(jnp.bfloat16)
        return total + partial_value.astype(jnp.float32)

    summed = lax.fori_loop(0, N_ROW, add_group, jnp.zeros((TOKENS, D), jnp.float32))
    grad_input = summed.astype(jnp.bfloat16)
    grad_weight = jnp.dot(inputs.T, grad_hidden, preferred_element_type=jnp.float32).astype(jnp.bfloat16)
    return grad_input, grad_weight
```

```python
import functools

import jax
import jax.numpy as jnp
from jax import lax
from jax.experimental import pallas as pl
from jax.experimental.pallas import tpu as pltpu
from jax.sharding import PartitionSpec as P

BF = jnp.bfloat16
F32 = jnp.float32
SIDE = 4
TILE = 768
WHOLE = pl.BlockSpec(memory_space=pltpu.VMEM)
FAR = pl.BlockSpec(memory_space=pltpu.HBM)
CHEAP = pl.CostEstimate(flops=1, bytes_accessed=1, transcendentals=0)


def gelu_slope(value):
    coeff = 0.7978845608
    inner = coeff * (value + 0.044715 * value * value * value)
    tanh_u = jnp.tanh(inner)
    return 0.5 * (1.0 + tanh_u) + 0.5 * value * (1.0 - tanh_u * tanh_u) * coeff * (
        1.0 + 3.0 * 0.044715 * value * value
    )


def hidden_cotangent(pre_values, out_values):
    return (out_values.astype(F32) * gelu_slope(pre_values.astype(F32))).astype(BF)


def move(array, step):
    pairs = []
    for x in range(SIDE):
        for z in range(SIDE):
            for y in range(SIDE):
                for c in range(2):
                    to_x, to_y, to_z, to_c = step(x, y, z, c)
                    to = ((to_x % SIDE * SIDE + to_z % SIDE) * SIDE + to_y % SIDE) * 2 + to_c
                    pairs.append((((x * SIDE + z) * SIDE + y) * 2 + c, to))
    return lax.ppermute(array, ("row", "col"), pairs)


def ring(array):
    return move(array, lambda x, y, z, c: (x, y + 1 - 2 * c, z, c))


def swap_core(array):
    return move(array, lambda x, y, z, c: (x, y, z, 1 - c))


def near(array, by):
    return move(array, lambda x, y, z, c: (x + by * c, y, z + by * (1 - c), c))


def far(array, by):
    return move(array, lambda x, y, z, c: (x + by * (1 - c), y, z + by * c, c))


def after(value, *others):
    return lax.optimization_barrier((value, *others))[0]


def fetch_kernel(source, target, sem):
    copy = pltpu.make_async_copy(source, target, sem)
    copy.start()
    copy.wait()


def fetch(array):
    return pl.pallas_call(
        fetch_kernel,
        out_shape=pltpu.VMEM(array.shape, array.dtype),
        in_specs=[FAR],
        out_specs=WHOLE,
        scratch_shapes=[pltpu.SemaphoreType.DMA],
        compiler_params=pltpu.CompilerParams(vmem_limit_bytes=12 * 2**20),
        cost_estimate=CHEAP,
    )(pltpu.with_memory_space_constraint(array, pltpu.HBM))


def partial_kernel(hops, has_store, *refs):
    count = 2 * len(hops)
    blocks, weight = refs[:count], refs[count]
    refs = refs[count + 1 :]
    if has_store:
        refs = refs[1 + SIDE :]
    store, outs, rows, sems = refs[0], refs[1 : 1 + SIDE], refs[-2], refs[-1]
    x, z = lax.axis_index("row") // SIDE, lax.axis_index("row") % SIDE
    y, c = lax.axis_index("col") // 2, lax.axis_index("col") % 2
    tokens = blocks[0].shape[1]
    places, copies = [], []
    for i, hop in enumerate(hops):
        for other in range(2):
            owner = 1 - c if other else c
            to_x = lax.rem(y + SIDE + jnp.where(owner == 0, -hop, hop), SIDE)
            for h in range(2):
                to_z = 2 * owner + h
                x_off, z_off = lax.rem(to_x + SIDE - x, SIDE), lax.rem(to_z + SIDE - z, SIDE)
                n_off, f_off = jnp.where(c == 0, z_off, x_off), jnp.where(c == 0, x_off, z_off)
                block, at = blocks[2 * i + other].at[h], len(places)
                copies.append(pltpu.make_async_copy(block, store.at[n_off, f_off], sems.at[at]))
                copies[-1].start()
                rows[at] = block[...]
                places.append((n_off, f_off))
    hidden = rows[...].reshape(len(places) * tokens, -1)
    for d in range(0, weight.shape[0], TILE):
        total = lax.dot_general(
            hidden, weight[d : d + TILE, :], (((1,), (1,)), ((), ())), preferred_element_type=F32
        ).astype(BF).reshape(len(places), tokens, TILE)
        for i, (n_off, f_off) in enumerate(places):
            for k in range(SIDE):

                @pl.when(n_off == k)
                def _():
                    outs[k][f_off, :, d : d + TILE] = total[i]

    for copy in copies:
        copy.wait()


def partial_input(hops, blocks, weight, store, outs):
    wide, hidden = weight.shape
    tokens = blocks[0].shape[1]
    given = [] if store is None else [store, *outs]
    first = len(blocks) + 1
    result = pl.pallas_call(
        functools.partial(partial_kernel, hops, bool(given)),
        out_shape=[pltpu.HBM((SIDE, SIDE, tokens, hidden), BF)]
        + [pltpu.VMEM((SIDE, tokens, wide), BF)] * SIDE,
        in_specs=[WHOLE] * first + ([FAR] + [WHOLE] * SIDE if given else []),
        out_specs=[FAR] + [WHOLE] * SIDE,
        scratch_shapes=[
            pltpu.VMEM((2 * len(blocks), tokens, hidden), BF),
            pltpu.SemaphoreType.DMA((2 * len(blocks),)),
        ],
        input_output_aliases={first + i: i for i in range(len(given))},
        compiler_params=pltpu.CompilerParams(vmem_limit_bytes=28 * 2**20),
        cost_estimate=CHEAP,
    )(*blocks, weight, *given)
    return result[0], list(result[1:])


def sum_kernel(*refs):
    terms, outs = refs[:SIDE], refs[SIDE:]
    for k in range(len(outs)):
        total = terms[0][k].astype(F32)
        for term in terms[1:]:
            total += term[k].astype(F32)
        outs[k][...] = total.astype(BF)


def sum_terms(terms):
    shape = terms[0].shape
    return pl.pallas_call(
        sum_kernel,
        out_shape=[pltpu.VMEM(shape[1:], BF)] * shape[0],
        in_specs=[WHOLE] * len(terms),
        out_specs=[WHOLE] * shape[0],
        cost_estimate=CHEAP,
    )(*terms)


def last_sum(terms):
    total = terms[0].astype(F32)
    for term in terms[1:]:
        total += term.astype(F32)
    return total.astype(BF)


def transpose_kernel(*refs):
    blocks, out, rows = refs[:SIDE], refs[SIDE], refs[SIDE + 1]
    tokens = blocks[0].shape[1]
    for n_off in range(SIDE):
        for f_off in range(SIDE):
            at = (n_off * SIDE + f_off) * tokens
            rows[at : at + tokens, :] = blocks[f_off][n_off]
    out[...] = rows[...].T


def transposed_inputs(blocks):
    _, tokens, wide = blocks[0].shape
    tokens *= SIDE * SIDE
    return pl.pallas_call(
        transpose_kernel,
        out_shape=pltpu.VMEM((wide, tokens), BF),
        in_specs=[WHOLE] * SIDE,
        out_specs=WHOLE,
        scratch_shapes=[pltpu.VMEM((tokens, wide), BF)],
        compiler_params=pltpu.CompilerParams(vmem_limit_bytes=24 * 2**20),
        cost_estimate=CHEAP,
    )(*blocks)


def weight_kernel(inputs_t, hidden, out):
    out[...] = jnp.dot(inputs_t[...], hidden[...], preferred_element_type=F32).astype(BF)


def weight_cotangent(inputs_t, hidden, tile=512):
    wide, tokens = inputs_t.shape
    units = hidden.shape[1]
    return pl.pallas_call(
        weight_kernel,
        grid=(units // tile,),
        out_shape=jax.ShapeDtypeStruct((wide, units), BF),
        in_specs=[WHOLE, pl.BlockSpec((tokens, tile), lambda i: (0, i))],
        out_specs=pl.BlockSpec((wide, tile), lambda i: (0, i)),
        compiler_params=pltpu.CompilerParams(vmem_limit_bytes=30 * 2**20),
        cost_estimate=CHEAP,
    )(inputs_t, pltpu.with_memory_space_constraint(hidden, pltpu.HBM))


def on_device(inputs, pre_act, grad_out, weight):
    hop0 = hidden_cotangent(pre_act, grad_out).reshape(2, -1, pre_act.shape[1])
    hop1 = ring(hop0)
    held_weight = fetch(after(weight, hop0))
    beside = [inputs] + [near(inputs, -k) for k in (1, 2, 3)]

    hop1, held_weight, *beside = lax.optimization_barrier((hop1, held_weight, *beside))
    hop2 = ring(hop1)
    stacked = jnp.stack(beside)
    gathered = {0: stacked, 1: far(stacked, -1), 3: far(stacked, -3)}
    blocks = [hop0, swap_core(hop0), hop1, swap_core(hop1)]

    hop2, stacked, gathered[1], gathered[3], *blocks = lax.optimization_barrier(
        (hop2, stacked, gathered[1], gathered[3], *blocks)
    )
    hop3 = ring(hop2)
    gathered[2] = far(stacked, -2)
    store, outs = partial_input((0, 1, 2), [*blocks, hop2, swap_core(hop2)], held_weight, None, None)

    hop3, gathered[2], *outs = lax.optimization_barrier((hop3, gathered[2], *outs))
    store, outs = partial_input((3,), [hop3, swap_core(hop3)], held_weight, store, outs)
    terms = [outs[0]] + [near(outs[k], k) for k in (1, 2, 3)]

    inputs_t = transposed_inputs([gathered[k] for k in range(SIDE)])
    grad_weight = weight_cotangent(inputs_t, store.reshape(-1, store.shape[-1]))
    grad_weight, *terms = lax.optimization_barrier((grad_weight, *terms))
    sums = sum_terms(terms)
    grad_input = last_sum([sums[0]] + [far(sums[k], k) for k in (1, 2, 3)])
    return (grad_input, grad_weight)


def solution(mesh):
    return jax.shard_map(
        on_device,
        mesh=mesh,
        in_specs=(P("row", "col"), P("col", "row"), P("col", "row"), P("col", "row")),
        out_specs=(P("row", "col"), P("col", "row")),
        check_vma=False,
    )
```

```python
import functools

import jax
import jax.numpy as jnp
from jax import lax
from jax.experimental import pallas as pl
from jax.experimental.pallas import tpu as pltpu
from jax.sharding import PartitionSpec as P

BF = jnp.bfloat16
F32 = jnp.float32
SIDE = 4
TILE = 768
WHOLE = pl.BlockSpec(memory_space=pltpu.VMEM)
FAR = pl.BlockSpec(memory_space=pltpu.HBM)
CHEAP = pl.CostEstimate(flops=1, bytes_accessed=1, transcendentals=0)


def gelu_slope(value):
    coeff = 0.7978845608
    square = value * value
    tanh_u = jnp.tanh(value * (coeff + (coeff * 0.044715) * square))
    slope = value * (coeff + (3.0 * 0.044715 * coeff) * square)
    return (0.5 + 0.5 * tanh_u) * (1.0 + (1.0 - tanh_u) * slope)


def hidden_cotangent(pre_values, out_values):
    return (out_values.astype(F32) * gelu_slope(pre_values.astype(F32))).astype(BF)


def move(array, step):
    pairs = []
    for x in range(SIDE):
        for z in range(SIDE):
            for y in range(SIDE):
                for c in range(2):
                    to_x, to_y, to_z, to_c = step(x, y, z, c)
                    to = ((to_x % SIDE * SIDE + to_z % SIDE) * SIDE + to_y % SIDE) * 2 + to_c
                    pairs.append((((x * SIDE + z) * SIDE + y) * 2 + c, to))
    return lax.ppermute(array, ("row", "col"), pairs)


def ring(array, by=1):
    return move(array, lambda x, y, z, c: (x, y + by * (1 - 2 * c), z, c))


def swap_core(array):
    return move(array, lambda x, y, z, c: (x, y, z, 1 - c))


def near(array, by):
    return move(array, lambda x, y, z, c: (x + by * c, y, z + by * (1 - c), c))


def far(array, by):
    return move(array, lambda x, y, z, c: (x + by * (1 - c), y, z + by * c, c))


def after(value, *others):
    return lax.optimization_barrier((value, *others))[0]


def fetch_kernel(source, target, sem):
    copy = pltpu.make_async_copy(source, target, sem)
    copy.start()
    copy.wait()


def fetch(array):
    return pl.pallas_call(
        fetch_kernel,
        out_shape=pltpu.VMEM(array.shape, array.dtype),
        in_specs=[FAR],
        out_specs=WHOLE,
        scratch_shapes=[pltpu.SemaphoreType.DMA],
        compiler_params=pltpu.CompilerParams(vmem_limit_bytes=12 * 2**20),
        cost_estimate=CHEAP,
    )(pltpu.with_memory_space_constraint(array, pltpu.HBM))


def block_offset(hop, swapped, h):
    x, z = lax.axis_index("row") // SIDE, lax.axis_index("row") % SIDE
    y, c = lax.axis_index("col") // 2, lax.axis_index("col") % 2
    owner = 1 - c if swapped else c
    to_x, to_z = lax.rem(y + SIDE + jnp.where(owner == 0, -hop, hop), SIDE), 2 * owner + h
    x_off, z_off = lax.rem(to_x + SIDE - x, SIDE), lax.rem(to_z + SIDE - z, SIDE)
    return jnp.where(c == 0, z_off, x_off), jnp.where(c == 0, x_off, z_off)


def partial_kernel(keys, has_outs, *refs):
    blocks, weight = refs[: len(keys)], refs[len(keys)]
    outs, found = refs[-1 - SIDE : -1], refs[-1]
    tokens = outs[0].shape[1]
    hidden = jnp.concatenate([block[...].reshape(2 * tokens, -1) for block in blocks])
    for d in range(0, weight.shape[0], TILE):
        found[:, d : d + TILE] = lax.dot_general(
            hidden, weight[d : d + TILE, :], (((1,), (1,)), ((), ())), preferred_element_type=F32
        ).astype(BF)
    for i, key in enumerate(keys):
        for h in range(2):
            n_off, f_off = block_offset(*key, h)
            at = (2 * i + h) * tokens
            for k in range(SIDE):

                @pl.when(n_off == k)
                def _():
                    outs[k][f_off] = found[at : at + tokens, :]


def partial_input(keys, pieces, weight, outs):
    blocks = [pieces[key] for key in keys]
    tokens = blocks[0].shape[1]
    first = len(blocks) + 1
    return list(
        pl.pallas_call(
            functools.partial(partial_kernel, keys, bool(outs)),
            out_shape=[pltpu.VMEM((SIDE, tokens, weight.shape[0]), BF)] * SIDE,
            in_specs=[WHOLE] * (first + len(outs)),
            out_specs=[WHOLE] * SIDE,
            scratch_shapes=[pltpu.VMEM((2 * tokens * len(blocks), weight.shape[0]), BF)],
            input_output_aliases={first + i: i for i in range(len(outs))},
            compiler_params=pltpu.CompilerParams(vmem_limit_bytes=16 * 2**20),
            cost_estimate=CHEAP,
        )(*blocks, weight, *outs)
    )


def sum_kernel(*refs):
    terms, outs = refs[:SIDE], refs[SIDE:]
    for k in range(len(outs)):
        total = terms[0][k].astype(F32)
        for term in terms[1:]:
            total += term[k].astype(F32)
        outs[k][...] = total.astype(BF)


def sum_terms(terms):
    shape = terms[0].shape
    return pl.pallas_call(
        sum_kernel,
        out_shape=[pltpu.VMEM(shape[1:], BF)] * shape[0],
        in_specs=[WHOLE] * len(terms),
        out_specs=[WHOLE] * shape[0],
        compiler_params=pltpu.CompilerParams(vmem_limit_bytes=6 * 2**20),
        cost_estimate=CHEAP,
    )(*terms)


def last_sum(terms):
    total = terms[0].astype(F32)
    for term in terms[1:]:
        total += term.astype(F32)
    return total.astype(BF)


def transpose_kernel(keys, *refs):
    blocks, out, rows = refs[:SIDE], refs[SIDE], refs[SIDE + 1]
    tokens = blocks[0].shape[1]
    for i, key in enumerate(keys):
        for h in range(2):
            n_off, f_off = block_offset(*key, h)
            at = (2 * i + h) * tokens
            for k in range(SIDE):

                @pl.when(f_off == k)
                def _():
                    rows[at : at + tokens, :] = blocks[k][n_off]

    out[...] = rows[...].T


def transposed_inputs(keys, blocks):
    _, tokens, wide = blocks[0].shape
    tokens *= SIDE * SIDE
    return pl.pallas_call(
        functools.partial(transpose_kernel, keys),
        out_shape=pltpu.VMEM((wide, tokens), BF),
        in_specs=[WHOLE] * SIDE,
        out_specs=WHOLE,
        scratch_shapes=[pltpu.VMEM((tokens, wide), BF)],
        compiler_params=pltpu.CompilerParams(vmem_limit_bytes=16 * 2**20),
        cost_estimate=CHEAP,
    )(*blocks)


def weight_kernel(inputs_t, *refs):
    pieces, out = refs[:-1], refs[-1]
    tile = out.shape[1]
    columns = pl.ds(pl.multiple_of(pl.program_id(0) * tile, tile), tile)
    hidden = jnp.concatenate([piece[:, columns] for piece in pieces])
    out[...] = jnp.dot(inputs_t[...], hidden, preferred_element_type=F32).astype(BF)


def weight_cotangent(inputs_t, pieces, tile=512):
    wide, units = inputs_t.shape[0], pieces[0].shape[-1]
    pieces = [piece.reshape(-1, units) for piece in pieces]
    return pl.pallas_call(
        weight_kernel,
        grid=(units // tile,),
        out_shape=jax.ShapeDtypeStruct((wide, units), BF),
        in_specs=[WHOLE] * (1 + len(pieces)),
        out_specs=pl.BlockSpec((wide, tile), lambda i: (0, i)),
        compiler_params=pltpu.CompilerParams(vmem_limit_bytes=18 * 2**20),
        cost_estimate=CHEAP,
    )(inputs_t, *pieces)


def on_device(inputs, pre_act, grad_out, weight):
    barrier = lax.optimization_barrier
    hop0 = hidden_cotangent(pre_act, grad_out).reshape(2, -1, pre_act.shape[1])
    beside = [inputs] + [near(inputs, -k) for k in (1, 2, 3)]
    swap0 = swap_core(hop0)
    hop1 = ring(hop0)
    held_weight = fetch(after(weight, hop0))

    hop1, swap0, held_weight, *beside = barrier((hop1, swap0, held_weight, *beside))
    swap1 = swap_core(hop1)
    stacked = jnp.stack(beside)
    gathered = {0: stacked, 1: far(stacked, -1), 3: far(stacked, -3), 2: far(stacked, -2)}
    hop2 = ring(hop1)
    pieces = {(0, False): hop0, (0, True): swap0, (1, False): hop1}
    outs = partial_input([(0, False), (0, True)], pieces, held_weight, [])

    hop2, swap1, *outs = barrier((hop2, swap1, *outs))
    hop3 = ring(hop2)
    swap2 = swap_core(hop2)
    pieces |= {(1, True): swap1, (2, False): hop2}
    outs = partial_input([(1, False), (1, True)], pieces, held_weight, outs)

    hop3, swap2, gathered[1], gathered[3], *outs = barrier((hop3, swap2, gathered[1], gathered[3], *outs))
    swap3 = swap_core(hop3)
    pieces |= {(2, True): swap2, (3, False): hop3}
    outs = partial_input([(2, False), (2, True)], pieces, held_weight, outs)
    swap3, gathered[2], *outs = barrier((swap3, gathered[2], *outs))
    pieces |= {(3, True): swap3}
    outs = partial_input([(3, False), (3, True)], pieces, held_weight, outs)
    terms = [outs[0]] + [near(outs[k], k) for k in (1, 2, 3)]

    inputs_t = transposed_inputs(list(pieces), [gathered[k] for k in range(SIDE)])
    grad_weight = weight_cotangent(inputs_t, list(pieces.values()))
    grad_weight, *terms = barrier((grad_weight, *terms))
    sums = sum_terms(terms)
    grad_input = last_sum([sums[0]] + [far(sums[k], k) for k in (1, 2, 3)])
    return (grad_input, grad_weight)


def solution(mesh):
    return jax.shard_map(
        on_device,
        mesh=mesh,
        in_specs=(P("row", "col"), P("col", "row"), P("col", "row"), P("col", "row")),
        out_specs=(P("row", "col"), P("col", "row")),
        check_vma=False,
    )
```

```python
import functools

import jax
import jax.numpy as jnp
from jax import lax
from jax.experimental import pallas as pl
from jax.experimental.pallas import tpu as pltpu
from jax.sharding import PartitionSpec as P

BF = jnp.bfloat16
F32 = jnp.float32
SIDE = 4
TILE = 768
WHOLE = pl.BlockSpec(memory_space=pltpu.VMEM)
FAR = pl.BlockSpec(memory_space=pltpu.HBM)
CHEAP = pl.CostEstimate(flops=1, bytes_accessed=1, transcendentals=0)


def gelu_slope(value):
    coeff = 0.7978845608
    square = value * value
    tanh_u = jnp.tanh(value * (coeff + (coeff * 0.044715) * square))
    slope = value * (coeff + (3.0 * 0.044715 * coeff) * square)
    return (0.5 + 0.5 * tanh_u) * (1.0 + (1.0 - tanh_u) * slope)


def hidden_cotangent(pre_values, out_values):
    return (out_values.astype(F32) * gelu_slope(pre_values.astype(F32))).astype(BF)


def move(array, step):
    pairs = []
    for x in range(SIDE):
        for z in range(SIDE):
            for y in range(SIDE):
                for c in range(2):
                    to_x, to_y, to_z, to_c = step(x, y, z, c)
                    to = ((to_x % SIDE * SIDE + to_z % SIDE) * SIDE + to_y % SIDE) * 2 + to_c
                    pairs.append((((x * SIDE + z) * SIDE + y) * 2 + c, to))
    return lax.ppermute(array, ("row", "col"), pairs)


def ring(array, by=1):
    return move(array, lambda x, y, z, c: (x, y + by * (1 - 2 * c), z, c))


def swap_core(array):
    return move(array, lambda x, y, z, c: (x, y, z, 1 - c))


def near(array, by):
    return move(array, lambda x, y, z, c: (x + by * c, y, z + by * (1 - c), c))


def far(array, by):
    return move(array, lambda x, y, z, c: (x + by * (1 - c), y, z + by * c, c))


def after(value, *others):
    return lax.optimization_barrier((value, *others))[0]


def passed(array):
    anywhere = pl.BlockSpec(memory_space=pl.ANY)
    return pl.pallas_call(
        lambda given, same: None,
        out_shape=jax.ShapeDtypeStruct(array.shape, array.dtype),
        in_specs=[anywhere],
        out_specs=anywhere,
        input_output_aliases={0: 0},
        compiler_params=pltpu.CompilerParams(vmem_limit_bytes=2**20),
        cost_estimate=pl.CostEstimate(flops=0, bytes_accessed=6 * 2**20, transcendentals=0),
    )(array)


def fetch_kernel(source, target, sem):
    copy = pltpu.make_async_copy(source, target, sem)
    copy.start()
    copy.wait()


def fetch(array):
    return pl.pallas_call(
        fetch_kernel,
        out_shape=pltpu.VMEM(array.shape, array.dtype),
        in_specs=[FAR],
        out_specs=WHOLE,
        scratch_shapes=[pltpu.SemaphoreType.DMA],
        compiler_params=pltpu.CompilerParams(vmem_limit_bytes=12 * 2**20),
        cost_estimate=CHEAP,
    )(pltpu.with_memory_space_constraint(array, pltpu.HBM))


def block_offset(hop, swapped, h):
    x, z = lax.axis_index("row") // SIDE, lax.axis_index("row") % SIDE
    y, c = lax.axis_index("col") // 2, lax.axis_index("col") % 2
    owner = 1 - c if swapped else c
    to_x, to_z = lax.rem(y + SIDE + jnp.where(owner == 0, -hop, hop), SIDE), 2 * owner + h
    x_off, z_off = lax.rem(to_x + SIDE - x, SIDE), lax.rem(to_z + SIDE - z, SIDE)
    return jnp.where(c == 0, z_off, x_off), jnp.where(c == 0, x_off, z_off)


def partial_kernel(keys, has_outs, *refs):
    blocks, weight = refs[: len(keys)], refs[len(keys)]
    outs, found = refs[-1 - SIDE : -1], refs[-1]
    tokens = outs[0].shape[1]
    hidden = jnp.concatenate([block[...].reshape(2 * tokens, -1) for block in blocks])
    for d in range(0, weight.shape[0], TILE):
        found[:, d : d + TILE] = lax.dot_general(
            hidden, weight[d : d + TILE, :], (((1,), (1,)), ((), ())), preferred_element_type=F32
        ).astype(BF)
    for i, key in enumerate(keys):
        for h in range(2):
            n_off, f_off = block_offset(*key, h)
            at = (2 * i + h) * tokens
            for k in range(SIDE):

                @pl.when(n_off == k)
                def _():
                    outs[k][f_off] = found[at : at + tokens, :]


def partial_input(keys, pieces, weight, outs):
    blocks = [pieces[key] for key in keys]
    tokens = blocks[0].shape[1]
    first = len(blocks) + 1
    return list(
        pl.pallas_call(
            functools.partial(partial_kernel, keys, bool(outs)),
            out_shape=[pltpu.VMEM((SIDE, tokens, weight.shape[0]), BF)] * SIDE,
            in_specs=[WHOLE] * (first + len(outs)),
            out_specs=[WHOLE] * SIDE,
            scratch_shapes=[pltpu.VMEM((2 * tokens * len(blocks), weight.shape[0]), BF)],
            input_output_aliases={first + i: i for i in range(len(outs))},
            compiler_params=pltpu.CompilerParams(vmem_limit_bytes=16 * 2**20),
            cost_estimate=CHEAP,
        )(*blocks, weight, *outs)
    )


def sum_kernel(*refs):
    terms, outs = refs[:SIDE], refs[SIDE:]
    for k in range(len(outs)):
        total = terms[0][k].astype(F32)
        for term in terms[1:]:
            total += term[k].astype(F32)
        outs[k][...] = total.astype(BF)


def sum_terms(terms):
    shape = terms[0].shape
    return pl.pallas_call(
        sum_kernel,
        out_shape=[pltpu.VMEM(shape[1:], BF)] * shape[0],
        in_specs=[WHOLE] * len(terms),
        out_specs=[WHOLE] * shape[0],
        compiler_params=pltpu.CompilerParams(vmem_limit_bytes=6 * 2**20),
        cost_estimate=CHEAP,
    )(*terms)


def last_sum(terms):
    total = terms[0].astype(F32)
    for term in terms[1:]:
        total += term.astype(F32)
    return total.astype(BF)


def transpose_kernel(keys, *refs):
    blocks, out, rows = refs[:SIDE], refs[SIDE], refs[SIDE + 1]
    tokens = blocks[0].shape[1]
    for i, key in enumerate(keys):
        for h in range(2):
            n_off, f_off = block_offset(*key, h)
            at = (2 * i + h) * tokens
            for k in range(SIDE):

                @pl.when(f_off == k)
                def _():
                    rows[at : at + tokens, :] = blocks[k][n_off]

    out[...] = rows[...].T


def transposed_inputs(keys, blocks):
    _, tokens, wide = blocks[0].shape
    tokens *= SIDE * SIDE
    return pl.pallas_call(
        functools.partial(transpose_kernel, keys),
        out_shape=pltpu.VMEM((wide, tokens), BF),
        in_specs=[WHOLE] * SIDE,
        out_specs=WHOLE,
        scratch_shapes=[pltpu.VMEM((tokens, wide), BF)],
        compiler_params=pltpu.CompilerParams(vmem_limit_bytes=16 * 2**20),
        cost_estimate=CHEAP,
    )(*blocks)


def weight_kernel(inputs_t, *refs):
    pieces, out = refs[:-1], refs[-1]
    tile = out.shape[1]
    columns = pl.ds(pl.multiple_of(pl.program_id(0) * tile, tile), tile)
    hidden = jnp.concatenate([piece[:, columns] for piece in pieces])
    out[...] = jnp.dot(inputs_t[...], hidden, preferred_element_type=F32).astype(BF)


def weight_cotangent(inputs_t, pieces, tile=512):
    wide, units = inputs_t.shape[0], pieces[0].shape[-1]
    pieces = [piece.reshape(-1, units) for piece in pieces]
    return pl.pallas_call(
        weight_kernel,
        grid=(units // tile,),
        out_shape=jax.ShapeDtypeStruct((wide, units), BF),
        in_specs=[WHOLE] * (1 + len(pieces)),
        out_specs=pl.BlockSpec((wide, tile), lambda i: (0, i)),
        compiler_params=pltpu.CompilerParams(vmem_limit_bytes=18 * 2**20),
        cost_estimate=CHEAP,
    )(inputs_t, *pieces)


def on_device(inputs, pre_act, grad_out, weight):
    barrier = lax.optimization_barrier
    hop0 = hidden_cotangent(pre_act, grad_out).reshape(2, -1, pre_act.shape[1])
    beside = [inputs] + [near(inputs, -k) for k in (1, 2, 3)]
    swap0 = swap_core(hop0)
    hop1 = ring(hop0)
    held_weight = fetch(after(weight, hop0))

    swap0, hop1, held_weight, *beside = barrier((swap0, hop1, held_weight, *beside))
    swap1 = swap_core(hop1)
    stacked = jnp.stack(beside)
    gathered = {0: stacked, 1: far(stacked, -1), 3: far(stacked, -3), 2: far(stacked, -2)}
    hop3 = ring(after(hop0, hop1), -1)
    hop2 = ring(hop1)
    pieces = {(0, False): hop0, (0, True): swap0, (1, False): hop1}
    outs = partial_input([(0, False), (0, True)], pieces, held_weight, [])

    swap1, *outs = barrier((swap1, *outs))
    pieces |= {(1, True): swap1}
    outs = partial_input([(1, False), (1, True)], pieces, held_weight, outs)

    hop3, hop2, *outs = barrier((hop3, hop2, *outs))
    swap2, swap3 = swap_core(hop2), swap_core(hop3)
    pieces |= {(2, False): hop2, (3, False): hop3}
    outs = partial_input([(2, False), (3, False)], pieces, held_weight, outs)
    gathered[2], gathered[3], gathered[1], *outs = barrier((gathered[2], gathered[3], gathered[1], *outs))
    gathered[2] = passed(gathered[2])

    swap2, swap3, gathered[2], *outs = barrier((swap2, swap3, gathered[2], *outs))
    pieces |= {(2, True): swap2, (3, True): swap3}
    outs = partial_input([(2, True), (3, True)], pieces, held_weight, outs)
    terms = [outs[0]] + [near(outs[k], k) for k in (1, 2, 3)]

    inputs_t = transposed_inputs(list(pieces), [gathered[k] for k in range(SIDE)])
    grad_weight = weight_cotangent(inputs_t, list(pieces.values()))
    grad_weight, *terms = barrier((grad_weight, *terms))
    sums = sum_terms(terms)
    grad_input = last_sum([sums[0]] + [far(sums[k], k) for k in (1, 2, 3)])
    return (grad_input, grad_weight)


def solution(mesh):
    return jax.shard_map(
        on_device,
        mesh=mesh,
        in_specs=(P("row", "col"), P("col", "row"), P("col", "row"), P("col", "row")),
        out_specs=(P("row", "col"), P("col", "row")),
        check_vma=False,
    )
```

```python
import functools

import jax
import jax.numpy as jnp
from jax import lax
from jax.experimental import pallas as pl
from jax.experimental.pallas import tpu as pltpu
from jax.sharding import PartitionSpec as P

BF = jnp.bfloat16
F32 = jnp.float32
SIDE = 4
TILE = 768
LOADS = 4
WHOLE = pl.BlockSpec(memory_space=pltpu.VMEM)
FAR = pl.BlockSpec(memory_space=pltpu.HBM)
CHEAP = pl.CostEstimate(flops=1, bytes_accessed=1, transcendentals=0)


def gelu_slope(value):
    coeff = 0.7978845608
    square = value * value
    tanh_u = jnp.tanh(value * (coeff + (coeff * 0.044715) * square))
    slope = value * (coeff + (3.0 * 0.044715 * coeff) * square)
    return (0.5 + 0.5 * tanh_u) * (1.0 + (1.0 - tanh_u) * slope)


def hidden_kernel(pre_act, grad_out, out, pre_held, grad_held, sems):
    width = out.shape[1] // LOADS
    loads = []
    for i in range(LOADS):
        columns = pl.ds(i * width, width)
        for j, (source, held) in enumerate(((pre_act, pre_held), (grad_out, grad_held))):
            loads.append(pltpu.make_async_copy(source.at[:, columns], held.at[:, columns], sems.at[j, i]))
            loads[-1].start()
    for i in range(LOADS):
        loads[2 * i].wait()
        loads[2 * i + 1].wait()
        for at in range(i * width, (i + 1) * width, 256):
            columns = pl.ds(at, 256)
            slope = gelu_slope(pre_held[:, columns].astype(F32))
            out[:, columns] = (grad_held[:, columns].astype(F32) * slope).astype(BF)


def hidden_cotangent(pre_act, grad_out):
    shape = pre_act.shape
    return pl.pallas_call(
        hidden_kernel,
        out_shape=pltpu.VMEM(shape, BF),
        in_specs=[FAR, FAR],
        out_specs=WHOLE,
        scratch_shapes=[pltpu.VMEM(shape, BF), pltpu.VMEM(shape, BF), pltpu.SemaphoreType.DMA((2, LOADS))],
        compiler_params=pltpu.CompilerParams(vmem_limit_bytes=8 * 2**20),
        cost_estimate=CHEAP,
    )(
        pltpu.with_memory_space_constraint(pre_act, pltpu.HBM),
        pltpu.with_memory_space_constraint(grad_out, pltpu.HBM),
    )


def move(array, step):
    pairs = []
    for x in range(SIDE):
        for z in range(SIDE):
            for y in range(SIDE):
                for c in range(2):
                    to_x, to_y, to_z, to_c = step(x, y, z, c)
                    to = ((to_x % SIDE * SIDE + to_z % SIDE) * SIDE + to_y % SIDE) * 2 + to_c
                    pairs.append((((x * SIDE + z) * SIDE + y) * 2 + c, to))
    return lax.ppermute(array, ("row", "col"), pairs)


def ring(array, by=1):
    return move(array, lambda x, y, z, c: (x, y + by * (1 - 2 * c), z, c))


def swap_core(array):
    return move(array, lambda x, y, z, c: (x, y, z, 1 - c))


def near(array, by):
    return move(array, lambda x, y, z, c: (x + by * c, y, z + by * (1 - c), c))


def far(array, by):
    return move(array, lambda x, y, z, c: (x + by * (1 - c), y, z + by * c, c))


def after(value, *others):
    return lax.optimization_barrier((value, *others))[0]


def passed(array):
    anywhere = pl.BlockSpec(memory_space=pl.ANY)
    return pl.pallas_call(
        lambda given, same: None,
        out_shape=jax.ShapeDtypeStruct(array.shape, array.dtype),
        in_specs=[anywhere],
        out_specs=anywhere,
        input_output_aliases={0: 0},
        compiler_params=pltpu.CompilerParams(vmem_limit_bytes=2**20),
        cost_estimate=pl.CostEstimate(flops=0, bytes_accessed=6 * 2**20, transcendentals=0),
    )(array)


def fetch_kernel(source, target, sem):
    copy = pltpu.make_async_copy(source, target, sem)
    copy.start()
    copy.wait()


def fetch(array):
    return pl.pallas_call(
        fetch_kernel,
        out_shape=pltpu.VMEM(array.shape, array.dtype),
        in_specs=[FAR],
        out_specs=WHOLE,
        scratch_shapes=[pltpu.SemaphoreType.DMA],
        compiler_params=pltpu.CompilerParams(vmem_limit_bytes=12 * 2**20),
        cost_estimate=CHEAP,
    )(pltpu.with_memory_space_constraint(array, pltpu.HBM))


def block_offset(hop, swapped, h):
    x, z = lax.axis_index("row") // SIDE, lax.axis_index("row") % SIDE
    y, c = lax.axis_index("col") // 2, lax.axis_index("col") % 2
    owner = 1 - c if swapped else c
    to_x, to_z = lax.rem(y + SIDE + jnp.where(owner == 0, -hop, hop), SIDE), 2 * owner + h
    x_off, z_off = lax.rem(to_x + SIDE - x, SIDE), lax.rem(to_z + SIDE - z, SIDE)
    return jnp.where(c == 0, z_off, x_off), jnp.where(c == 0, x_off, z_off)


def partial_kernel(keys, has_outs, *refs):
    blocks, weight = refs[: len(keys)], refs[len(keys)]
    outs, found = refs[-1 - SIDE : -1], refs[-1]
    tokens = outs[0].shape[1]
    hidden = jnp.concatenate([block[...].reshape(2 * tokens, -1) for block in blocks])
    for d in range(0, weight.shape[0], TILE):
        found[:, d : d + TILE] = lax.dot_general(
            hidden, weight[d : d + TILE, :], (((1,), (1,)), ((), ())), preferred_element_type=F32
        ).astype(BF)
    for i, key in enumerate(keys):
        for h in range(2):
            n_off, f_off = block_offset(*key, h)
            at = (2 * i + h) * tokens
            for k in range(SIDE):

                @pl.when(n_off == k)
                def _():
                    outs[k][f_off] = found[at : at + tokens, :]


def partial_input(keys, pieces, weight, outs):
    blocks = [pieces[key] for key in keys]
    tokens = blocks[0].shape[1]
    first = len(blocks) + 1
    return list(
        pl.pallas_call(
            functools.partial(partial_kernel, keys, bool(outs)),
            out_shape=[pltpu.VMEM((SIDE, tokens, weight.shape[0]), BF)] * SIDE,
            in_specs=[WHOLE] * (first + len(outs)),
            out_specs=[WHOLE] * SIDE,
            scratch_shapes=[pltpu.VMEM((2 * tokens * len(blocks), weight.shape[0]), BF)],
            input_output_aliases={first + i: i for i in range(len(outs))},
            compiler_params=pltpu.CompilerParams(vmem_limit_bytes=16 * 2**20),
            cost_estimate=CHEAP,
        )(*blocks, weight, *outs)
    )


def sum_kernel(*refs):
    terms, outs = refs[:SIDE], refs[SIDE:]
    for k in range(len(outs)):
        total = terms[0][k].astype(F32)
        for term in terms[1:]:
            total += term[k].astype(F32)
        outs[k][...] = total.astype(BF)


def sum_terms(terms):
    shape = terms[0].shape
    return pl.pallas_call(
        sum_kernel,
        out_shape=[pltpu.VMEM(shape[1:], BF)] * shape[0],
        in_specs=[WHOLE] * len(terms),
        out_specs=[WHOLE] * shape[0],
        compiler_params=pltpu.CompilerParams(vmem_limit_bytes=6 * 2**20),
        cost_estimate=CHEAP,
    )(*terms)


def last_sum(terms):
    total = terms[0].astype(F32)
    for term in terms[1:]:
        total += term.astype(F32)
    return total.astype(BF)


def transpose_kernel(keys, *refs):
    blocks, out, rows = refs[:SIDE], refs[SIDE], refs[SIDE + 1]
    tokens = blocks[0].shape[1]
    for i, key in enumerate(keys):
        for h in range(2):
            n_off, f_off = block_offset(*key, h)
            at = (2 * i + h) * tokens
            for k in range(SIDE):

                @pl.when(f_off == k)
                def _():
                    rows[at : at + tokens, :] = blocks[k][n_off]

    out[...] = rows[...].T


def transposed_inputs(keys, blocks):
    _, tokens, wide = blocks[0].shape
    tokens *= SIDE * SIDE
    return pl.pallas_call(
        functools.partial(transpose_kernel, keys),
        out_shape=pltpu.VMEM((wide, tokens), BF),
        in_specs=[WHOLE] * SIDE,
        out_specs=WHOLE,
        scratch_shapes=[pltpu.VMEM((tokens, wide), BF)],
        compiler_params=pltpu.CompilerParams(vmem_limit_bytes=16 * 2**20),
        cost_estimate=CHEAP,
    )(*blocks)


def weight_kernel(inputs_t, *refs):
    pieces, out = refs[:-1], refs[-1]
    tile = out.shape[1]
    columns = pl.ds(pl.multiple_of(pl.program_id(0) * tile, tile), tile)
    hidden = jnp.concatenate([piece[:, columns] for piece in pieces])
    out[...] = jnp.dot(inputs_t[...], hidden, preferred_element_type=F32).astype(BF)


def weight_cotangent(inputs_t, pieces, tile=512):
    wide, units = inputs_t.shape[0], pieces[0].shape[-1]
    pieces = [piece.reshape(-1, units) for piece in pieces]
    return pl.pallas_call(
        weight_kernel,
        grid=(units // tile,),
        out_shape=jax.ShapeDtypeStruct((wide, units), BF),
        in_specs=[WHOLE] * (1 + len(pieces)),
        out_specs=pl.BlockSpec((wide, tile), lambda i: (0, i)),
        compiler_params=pltpu.CompilerParams(vmem_limit_bytes=18 * 2**20),
        cost_estimate=CHEAP,
    )(inputs_t, *pieces)


def on_device(inputs, pre_act, grad_out, weight):
    barrier = lax.optimization_barrier
    hop0 = hidden_cotangent(pre_act, grad_out).reshape(2, -1, pre_act.shape[1])
    beside = [inputs] + [near(inputs, -k) for k in (1, 2, 3)]
    swap0 = swap_core(hop0)
    hop1 = ring(hop0)
    held_weight = fetch(after(weight, hop0))

    swap0, hop1, held_weight, *beside = barrier((swap0, hop1, held_weight, *beside))
    swap1 = swap_core(hop1)
    stacked = jnp.stack(beside)
    gathered = {0: stacked, 1: far(stacked, -1), 3: far(stacked, -3), 2: far(stacked, -2)}
    hop3 = ring(after(hop0, hop1), -1)
    hop2 = ring(hop1)
    pieces = {(0, False): hop0, (0, True): swap0, (1, False): hop1}
    outs = partial_input([(0, False), (0, True)], pieces, held_weight, [])

    swap1, *outs = barrier((swap1, *outs))
    pieces |= {(1, True): swap1}
    outs = partial_input([(1, False), (1, True)], pieces, held_weight, outs)

    hop3, hop2, *outs = barrier((hop3, hop2, *outs))
    swap2, swap3 = swap_core(hop2), swap_core(hop3)
    pieces |= {(2, False): hop2, (3, False): hop3}
    outs = partial_input([(2, False), (3, False)], pieces, held_weight, outs)
    gathered[2], gathered[3], gathered[1], *outs = barrier((gathered[2], gathered[3], gathered[1], *outs))
    gathered[2] = passed(gathered[2])

    swap2, swap3, gathered[2], *outs = barrier((swap2, swap3, gathered[2], *outs))
    pieces |= {(2, True): swap2, (3, True): swap3}
    outs = partial_input([(2, True), (3, True)], pieces, held_weight, outs)
    terms = [outs[0]] + [near(outs[k], k) for k in (1, 2, 3)]

    inputs_t = transposed_inputs(list(pieces), [gathered[k] for k in range(SIDE)])
    grad_weight = weight_cotangent(inputs_t, list(pieces.values()))
    grad_weight, *terms = barrier((grad_weight, *terms))
    sums = sum_terms(terms)
    grad_input = last_sum([sums[0]] + [far(sums[k], k) for k in (1, 2, 3)])
    return (grad_input, grad_weight)


def solution(mesh):
    return jax.shard_map(
        on_device,
        mesh=mesh,
        in_specs=(P("row", "col"), P("col", "row"), P("col", "row"), P("col", "row")),
        out_specs=(P("row", "col"), P("col", "row")),
        check_vma=False,
    )
```

```python
import functools

import jax
import jax.numpy as jnp
from jax import lax
from jax.experimental import pallas as pl
from jax.experimental.pallas import tpu as pltpu
from jax.sharding import PartitionSpec as P

BF = jnp.bfloat16
F32 = jnp.float32
SIDE = 4
TILE = 768
LOADS = 4
WHOLE = pl.BlockSpec(memory_space=pltpu.VMEM)
FAR = pl.BlockSpec(memory_space=pltpu.HBM)
CHEAP = pl.CostEstimate(flops=1, bytes_accessed=1, transcendentals=0)


def gelu_slope(value):
    coeff = 0.7978845608
    square = value * value
    tanh_u = jnp.tanh(value * (coeff + (coeff * 0.044715) * square))
    slope = value * (coeff + (3.0 * 0.044715 * coeff) * square)
    return (0.5 + 0.5 * tanh_u) * (1.0 + (1.0 - tanh_u) * slope)


def hidden_kernel(pre_act, grad_out, out, pre_held, grad_held, sems):
    width = out.shape[1] // LOADS
    loads = []
    for i in range(LOADS):
        columns = pl.ds(i * width, width)
        for j, (source, held) in enumerate(((pre_act, pre_held), (grad_out, grad_held))):
            loads.append(pltpu.make_async_copy(source.at[:, columns], held.at[:, columns], sems.at[j, i]))
            loads[-1].start()
    for i in range(LOADS):
        loads[2 * i].wait()
        loads[2 * i + 1].wait()
        for at in range(i * width, (i + 1) * width, 256):
            columns = pl.ds(at, 256)
            slope = gelu_slope(pre_held[:, columns].astype(F32))
            out[:, columns] = (grad_held[:, columns].astype(F32) * slope).astype(BF)


def hidden_cotangent(pre_act, grad_out):
    shape = pre_act.shape
    return pl.pallas_call(
        hidden_kernel,
        out_shape=pltpu.VMEM(shape, BF),
        in_specs=[FAR, FAR],
        out_specs=WHOLE,
        scratch_shapes=[pltpu.VMEM(shape, BF), pltpu.VMEM(shape, BF), pltpu.SemaphoreType.DMA((2, LOADS))],
        compiler_params=pltpu.CompilerParams(vmem_limit_bytes=8 * 2**20),
        cost_estimate=CHEAP,
    )(
        pltpu.with_memory_space_constraint(pre_act, pltpu.HBM),
        pltpu.with_memory_space_constraint(grad_out, pltpu.HBM),
    )


def move(array, step):
    pairs = []
    for x in range(SIDE):
        for z in range(SIDE):
            for y in range(SIDE):
                for c in range(2):
                    to_x, to_y, to_z, to_c = step(x, y, z, c)
                    to = ((to_x % SIDE * SIDE + to_z % SIDE) * SIDE + to_y % SIDE) * 2 + to_c
                    pairs.append((((x * SIDE + z) * SIDE + y) * 2 + c, to))
    return lax.ppermute(array, ("row", "col"), pairs)


def ring(array, by=1):
    return move(array, lambda x, y, z, c: (x, y + by * (1 - 2 * c), z, c))


def swap_core(array):
    return move(array, lambda x, y, z, c: (x, y, z, 1 - c))


def near(array, by):
    return move(array, lambda x, y, z, c: (x + by * c, y, z + by * (1 - c), c))


def far(array, by):
    return move(array, lambda x, y, z, c: (x + by * (1 - c), y, z + by * c, c))


def after(value, *others):
    return lax.optimization_barrier((value, *others))[0]


def passed(array):
    anywhere = pl.BlockSpec(memory_space=pl.ANY)
    return pl.pallas_call(
        lambda given, same: None,
        out_shape=jax.ShapeDtypeStruct(array.shape, array.dtype),
        in_specs=[anywhere],
        out_specs=anywhere,
        input_output_aliases={0: 0},
        compiler_params=pltpu.CompilerParams(vmem_limit_bytes=2**20),
        cost_estimate=pl.CostEstimate(flops=0, bytes_accessed=6 * 2**20, transcendentals=0),
    )(array)


def fetch_kernel(source, target, sem):
    copy = pltpu.make_async_copy(source, target, sem)
    copy.start()
    copy.wait()


def fetch(array):
    return pl.pallas_call(
        fetch_kernel,
        out_shape=pltpu.VMEM(array.shape, array.dtype),
        in_specs=[FAR],
        out_specs=WHOLE,
        scratch_shapes=[pltpu.SemaphoreType.DMA],
        compiler_params=pltpu.CompilerParams(vmem_limit_bytes=12 * 2**20),
        cost_estimate=CHEAP,
    )(pltpu.with_memory_space_constraint(array, pltpu.HBM))


def block_offset(hop, swapped, h):
    x, z = lax.axis_index("row") // SIDE, lax.axis_index("row") % SIDE
    y, c = lax.axis_index("col") // 2, lax.axis_index("col") % 2
    owner = 1 - c if swapped else c
    to_x, to_z = lax.rem(y + SIDE + jnp.where(owner == 0, -hop, hop), SIDE), 2 * owner + h
    x_off, z_off = lax.rem(to_x + SIDE - x, SIDE), lax.rem(to_z + SIDE - z, SIDE)
    return jnp.where(c == 0, z_off, x_off), jnp.where(c == 0, x_off, z_off)


def partial_kernel(keys, has_outs, *refs):
    blocks, weight = refs[: len(keys)], refs[len(keys)]
    own, up, down, up_rest, down_rest, found = refs[-6:]
    tokens = own.shape[1]
    hidden = jnp.concatenate([block[...].reshape(2 * tokens, -1) for block in blocks])
    for d in range(0, weight.shape[0], TILE):
        found[:, d : d + TILE] = lax.dot_general(
            hidden, weight[d : d + TILE, :], (((1,), (1,)), ((), ())), preferred_element_type=F32
        ).astype(BF)
    for i, key in enumerate(keys):
        for h in range(2):
            n_off, f_off = block_offset(*key, h)
            at = (2 * i + h) * tokens
            low = f_off < 2
            for k, is_low, out, *index in (
                (1, True, up_rest, f_off),
                (1, False, up, 1, f_off - 2),
                (2, True, up, 0, f_off),
                (2, False, down, 0, f_off - 2),
                (3, True, down, 1, f_off),
                (3, False, down_rest, f_off - 2),
            ):

                @pl.when((n_off == k) & (low if is_low else ~low))
                def _():
                    out[tuple(index)] = found[at : at + tokens, :]

            @pl.when(n_off == 0)
            def _():
                own[f_off] = found[at : at + tokens, :]


def partial_input(keys, pieces, weight, outs):
    blocks = [pieces[key] for key in keys]
    tokens = blocks[0].shape[1]
    first = len(blocks) + 1
    return list(
        pl.pallas_call(
            functools.partial(partial_kernel, keys, bool(outs)),
            out_shape=[
                pltpu.VMEM((*lead, tokens, weight.shape[0]), BF) for lead in ((4,), (2, 2), (2, 2), (2,), (2,))
            ],
            in_specs=[WHOLE] * (first + len(outs)),
            out_specs=[WHOLE] * 5,
            scratch_shapes=[pltpu.VMEM((2 * tokens * len(blocks), weight.shape[0]), BF)],
            input_output_aliases={first + i: i for i in range(len(outs))},
            compiler_params=pltpu.CompilerParams(vmem_limit_bytes=16 * 2**20),
            cost_estimate=CHEAP,
        )(*blocks, weight, *outs)
    )


def rest_kernel(up_rest, down_rest, from_below, from_above, up, down):
    for rest, share, out in ((up_rest, from_below, up), (down_rest, from_above, down)):
        for i in range(2):
            out[i] = (rest[i].astype(F32) + share[0, i].astype(F32)).astype(BF)


def sum_kernel(own, from_below, from_above, last_below, last_above, *outs):
    for f in range(SIDE):
        direct, rest = (from_above, last_below) if f < 2 else (from_below, last_above)
        total = own[f].astype(F32) + direct[1, f % 2].astype(F32) + rest[f % 2].astype(F32)
        outs[f][...] = total.astype(BF)


def in_vmem(kernel, shapes, *operands):
    return pl.pallas_call(
        kernel,
        out_shape=[pltpu.VMEM(shape, BF) for shape in shapes],
        in_specs=[WHOLE] * len(operands),
        out_specs=[WHOLE] * len(shapes),
        compiler_params=pltpu.CompilerParams(vmem_limit_bytes=6 * 2**20),
        cost_estimate=CHEAP,
    )(*operands)


def last_sum(terms):
    total = terms[0].astype(F32)
    for term in terms[1:]:
        total += term.astype(F32)
    return total.astype(BF)


def transpose_kernel(keys, *refs):
    blocks, out, rows = refs[:SIDE], refs[SIDE], refs[SIDE + 1]
    tokens = blocks[0].shape[1]
    for i, key in enumerate(keys):
        for h in range(2):
            n_off, f_off = block_offset(*key, h)
            at = (2 * i + h) * tokens
            for k in range(SIDE):

                @pl.when(f_off == k)
                def _():
                    rows[at : at + tokens, :] = blocks[k][n_off]

    out[...] = rows[...].T


def transposed_inputs(keys, blocks):
    _, tokens, wide = blocks[0].shape
    tokens *= SIDE * SIDE
    return pl.pallas_call(
        functools.partial(transpose_kernel, keys),
        out_shape=pltpu.VMEM((wide, tokens), BF),
        in_specs=[WHOLE] * SIDE,
        out_specs=WHOLE,
        scratch_shapes=[pltpu.VMEM((tokens, wide), BF)],
        compiler_params=pltpu.CompilerParams(vmem_limit_bytes=16 * 2**20),
        cost_estimate=CHEAP,
    )(*blocks)


def weight_kernel(first, inputs_t, *refs):
    out = refs[-1]
    tile = out.shape[1]
    columns = pl.ds(pl.multiple_of((first + pl.program_id(0)) * tile, tile), tile)
    hidden = jnp.concatenate([piece[:, columns] for piece in refs[:8]])
    out[...] = jnp.dot(inputs_t[...], hidden, preferred_element_type=F32).astype(BF)


def weight_cotangent(inputs_t, pieces, first, count, done, tile=512):
    wide, units = inputs_t.shape[0], pieces[0].shape[-1]
    pieces = [piece.reshape(-1, units) for piece in pieces]
    return pl.pallas_call(
        functools.partial(weight_kernel, first),
        grid=(count,),
        out_shape=jax.ShapeDtypeStruct((wide, units), BF),
        in_specs=[WHOLE] * (1 + len(pieces)) + [FAR] * len(done),
        out_specs=pl.BlockSpec((wide, tile), lambda i: (0, first + i)),
        input_output_aliases={1 + len(pieces): 0} if done else {},
        compiler_params=pltpu.CompilerParams(vmem_limit_bytes=18 * 2**20),
        cost_estimate=CHEAP,
    )(inputs_t, *pieces, *done)


def on_device(inputs, pre_act, grad_out, weight):
    barrier = lax.optimization_barrier
    hop0 = hidden_cotangent(pre_act, grad_out).reshape(2, -1, pre_act.shape[1])
    beside = [inputs] + [near(inputs, -k) for k in (1, 2, 3)]
    swap0 = swap_core(hop0)
    hop1 = ring(hop0)
    held_weight = fetch(after(weight, hop0))

    swap0, hop1, held_weight, *beside = barrier((swap0, hop1, held_weight, *beside))
    swap1 = swap_core(hop1)
    stacked = jnp.stack(beside)
    gathered = {0: stacked, 1: far(stacked, -1), 3: far(stacked, -3), 2: far(stacked, -2)}
    hop3 = ring(after(hop0, hop1), -1)
    hop2 = ring(hop1)
    pieces = {(0, False): hop0, (0, True): swap0, (1, False): hop1}
    outs = partial_input([(0, False), (0, True)], pieces, held_weight, [])

    swap1, *outs = barrier((swap1, *outs))
    pieces |= {(1, True): swap1}
    outs = partial_input([(1, False), (1, True)], pieces, held_weight, outs)

    hop3, hop2, *outs = barrier((hop3, hop2, *outs))
    swap2, swap3 = swap_core(hop2), swap_core(hop3)
    pieces |= {(2, False): hop2, (3, False): hop3}
    outs = partial_input([(2, False), (3, False)], pieces, held_weight, outs)
    gathered[2], gathered[3], gathered[1], *outs = barrier((gathered[2], gathered[3], gathered[1], *outs))
    gathered[2] = passed(gathered[2])

    swap2, swap3, gathered[2], *outs = barrier((swap2, swap3, gathered[2], *outs))
    pieces |= {(2, True): swap2, (3, True): swap3}
    outs = partial_input([(2, True), (3, True)], pieces, held_weight, outs)
    own, up, down, up_rest, down_rest = outs
    from_below, from_above = near(up, 1), near(down, -1)

    inputs_t = transposed_inputs(list(pieces), [gathered[k] for k in range(SIDE)])
    pieces = list(pieces.values())
    grad_weight = weight_cotangent(inputs_t, pieces, 0, 3, [])
    grad_weight, from_below, from_above = barrier((grad_weight, from_below, from_above))
    up, down = in_vmem(rest_kernel, [up_rest.shape] * 2, up_rest, down_rest, from_below, from_above)
    last_below, last_above = near(up, 1), near(down, -1)
    grad_weight = weight_cotangent(inputs_t, pieces, 3, 2, [grad_weight])
    grad_weight, last_below, last_above = barrier((grad_weight, last_below, last_above))
    sums = in_vmem(sum_kernel, [own.shape[1:]] * SIDE, own, from_below, from_above, last_below, last_above)
    terms = [sums[0]] + [far(sums[k], k) for k in (1, 2, 3)]
    grad_weight = weight_cotangent(inputs_t, pieces, 5, 1, [grad_weight])
    grad_weight, *terms = barrier((grad_weight, *terms))
    grad_input = last_sum(terms)
    return (grad_input, grad_weight)


def solution(mesh):
    return jax.shard_map(
        on_device,
        mesh=mesh,
        in_specs=(P("row", "col"), P("col", "row"), P("col", "row"), P("col", "row")),
        out_specs=(P("row", "col"), P("col", "row")),
        check_vma=False,
    )
```
